32 devices in a mesh: row: 4 (over y, x), col: 8 (over z, core).
Axes of the slice: x: 2, y: 2, z: 4, core: 2. Of those that a mesh axis runs over, the one named last changes fastest.
Arguments:
- fingerprints: bfloat16 [8192, 1024], P(('row', 'col')), as said below
- probes: bfloat16 [8192, 256], P(('row', 'col')), may hold values from -6 to 6
Outputs:
- image: float32 [8192, 256], P(('row', 'col'))
The draws below stay inside these ranges and needn't reach their ends.
Inputs may be any that keep to these rules, and one draw needn't show every extreme that they name: `fingerprints`: every entry is positive.
All inputs are finite; a program needn't handle non-finite values.
Results may differ from the reference program's by a relative error of at most 0.0031.
Values may be sent and summed in bfloat16 or wider, within the bound.
A program may use at most 64 MiB of HBM per device.

```python
import math
import jax
import jax.numpy as jnp
from jax import lax

FEAT = 1024
PROBES = 256
M_DEV = 256
NTOT = 8192


def draw_fingerprints(key, part):
    first = jax.random.fold_in(key, 0)
    second = jax.random.fold_in(key, 1)
    third = jax.random.fold_in(key, 2)
    fourth = jax.random.fold_in(key, 3)
    sixth = jax.random.fold_in(key, 5)
    density = jnp.exp(jax.random.uniform(first, (NTOT, 1), jnp.float32, jnp.log(0.08), jnp.log(0.6)))
    present = (jax.random.uniform(second, (NTOT, FEAT), jnp.float32) < density).astype(jnp.float32)
    feature_weight = jnp.exp(jax.random.uniform(third, (1, FEAT), jnp.float32, jnp.log(0.8), jnp.log(1.25)))
    background = jax.random.uniform(sixth, (NTOT, FEAT), jnp.float32, 0.05, 1.0)
    counts = jnp.exp(jax.random.uniform(fourth, (NTOT, FEAT), jnp.float32, jnp.log(0.1), jnp.log(10.0)))
    return (feature_weight * counts * (present + background)).astype(jnp.bfloat16)


def level_of(rng, dims, shards, least, largest):
    gain, own = 1.0, jax.random.fold_in(rng, 6)
    for dim, blocks in shards:
        heights = jnp.exp(jax.random.uniform(jax.random.fold_in(own, dim), (blocks,), jnp.float32, least / len(shards), largest / len(shards)))
        gain = gain * jnp.repeat(heights, dims[dim] // blocks).reshape([-1 if axis == dim else 1 for axis in range(len(dims))])
    return gain


def scatter_about(rng, dims, scale, bound, cuts=(), held_as=jnp.bfloat16):
    loudness = level_of(rng, dims, cuts, -0.22, 0.18) if cuts else 1.0
    values = jax.random.normal(rng, dims, jnp.float32) * scale * loudness
    return jnp.minimum(jnp.maximum(values, -bound), bound).astype(held_as)


def setup_inputs(seed: int = 0) -> dict:
    splits = jax.random.split(jax.random.key(seed), 3)
    fingerprints = draw_fingerprints(jax.random.fold_in(splits[2], 71), 0)
    probes = scatter_about(splits[1], (NTOT, PROBES), 1.0, 6.0, ((0, 32),))
    return dict(fingerprints=fingerprints, probes=probes)


def reference(fingerprints, probes):
    values = fingerprints.astype(jnp.float32)
    sq = lax.optimization_barrier(jnp.sum(values * values, axis=1))
    weights = probes.astype(jnp.float32)
    blocks = values.reshape(NTOT // M_DEV, M_DEV, FEAT)
    block_sq = sq.reshape(NTOT // M_DEV, M_DEV)

    def one_block(pair):
        rows_now, rows_sq = pair
        inner = jnp.dot(rows_now, values.T, precision=lax.Precision.HIGHEST, preferred_element_type=jnp.float32)
        kernel = inner / (rows_sq[:, None] + sq[None, :] - inner)
        kernel = lax.optimization_barrier(kernel.astype(jnp.bfloat16)).astype(jnp.float32)
        return jnp.dot(kernel, weights, precision=lax.Precision.HIGHEST, preferred_element_type=jnp.float32)
    result = lax.map(one_block, (blocks, block_sq)).reshape(NTOT, PROBES)
    return result / math.sqrt(NTOT)
```

```python
import functools
import math

import jax
import jax.numpy as jnp
from jax import lax
from jax.experimental import pallas as pl
from jax.experimental.pallas import tpu as pltpu
from jax.sharding import PartitionSpec as P

MESH = pl.DeviceIdType.MESH
SENT = jnp.float32


def flip(index, pattern, size):
    result, weight = 0, 1
    while weight < size:
        result = result + weight * ((index // weight + pattern // weight) % 2)
        weight *= 2
    return result


def kernel(n_row, n_chip, factor, fp, pr, out, slab, cols, cpr, part, other, stage, ret, sq_first, sq_second,
           z_send, z_recv, s_send, s_recv, f_send, f_recv, p_send, p_recv, o_send, o_recv, r_send, r_recv):
    rows = fp.shape[0]
    row, col = lax.axis_index("row"), lax.axis_index("col")
    chip, core = col // 2, col % 2
    twin = col + 1 - 2 * core
    mine = pl.ds(pl.multiple_of(core * rows, rows), rows)
    others = pl.ds(pl.multiple_of((1 - core) * rows, rows), rows)

    def remote(src, dst, send, recv, where):
        return pltpu.make_async_remote_copy(
            src_ref=src, dst_ref=dst, send_sem=send, recv_sem=recv, device_id=where, device_id_type=MESH
        )

    def along(s, way, chip_to):
        return remote(slab.at[s, mine], slab.at[s, mine], z_send.at[way, s], z_recv.at[s], (row, 2 * chip_to + core))

    def to_twin(s, half):
        return remote(slab.at[s, half], slab.at[s, half], s_send.at[s], s_recv.at[s], (row, twin))

    def rows_to(p):
        peer = flip(row, p, n_row)
        return (
            remote(fp, cols.at[row], f_send.at[p], f_recv.at[p], (peer, col)),
            remote(pr, cpr.at[row], p_send.at[p], p_recv.at[p], (peer, col)),
        )

    def rows_from(p):
        peer = flip(row, p, n_row)
        return (
            remote(fp, cols.at[peer], f_send.at[p], f_recv.at[p], (peer, col)),
            remote(pr, cpr.at[peer], p_send.at[p], p_recv.at[p], (peer, col)),
        )

    def partial_to_twin(s):
        return remote(part.at[s, others], other.at[s], o_send.at[s], o_recv.at[s], (row, twin))

    def result_to(s):
        return remote(stage.at[s], ret.at[chip], r_send.at[s], r_recv.at[chip], (row, 2 * s + core))

    def result_from(s):
        return remote(stage.at[s], ret.at[s], r_send.at[s], r_recv.at[s], (row, 2 * s + core))

    def each(low, high, body):
        def step(i, carry):
            body(i)
            return carry
        lax.fori_loop(low, high, step, 0)

    barrier = pltpu.get_barrier_semaphore()

    def greet(where):
        pl.semaphore_signal(barrier, inc=1, device_id=where, device_id_type=MESH)

    each(1, n_row, lambda p: greet((flip(row, p, n_row), col)))
    each(1, n_chip, lambda d: greet((row, 2 * ((chip + d) % n_chip) + core)))
    greet((row, twin))
    slab[chip, mine] = fp[...]
    cols[row] = fp[...]
    cpr[row] = pr[...]
    pl.semaphore_wait(barrier, n_row - 1 + n_chip - 1 + 1)

    @pl.when(chip + 1 < n_chip)
    def _():
        along(chip, 0, chip + 1).start()

    @pl.when(chip > 0)
    def _():
        along(chip, 1, chip - 1).start()

    to_twin(chip, mine).start()

    def start_rows(p):
        for copy in rows_to(p):
            copy.start()
    each(1, n_row, start_rows)

    def prepare_first(s):
        values = slab[s].astype(jnp.float32)
        sq_first[s] = jnp.broadcast_to(jnp.sum(values * values, axis=1, keepdims=True), sq_first.shape[1:])

    def prepare_second(r):
        values = cols[r].astype(jnp.float32)
        total = jnp.broadcast_to(jnp.sum(values * values, axis=1, keepdims=True), (rows, 128))
        sq_second[r] = total.T[:8]

    def tile(s, r):
        inner = lax.dot_general(slab[s], cols[r], (((1,), (1,)), ((), ())), preferred_element_type=jnp.float32)
        value = inner / (sq_first[s][:, :1] + sq_second[r][:1] - inner)
        part[s] += jnp.dot(value.astype(jnp.bfloat16), cpr[r], preferred_element_type=jnp.float32)

    part[...] = jnp.zeros_like(part)
    prepare_second(row)
    to_twin(chip, others).wait_recv()
    prepare_first(chip)
    tile(chip, row)

    def receive(d, onward):
        @pl.when(chip - d >= 0)
        def _():
            along(chip - d, 0, chip).wait_recv()
            if onward:
                @pl.when(chip + 1 < n_chip)
                def _():
                    along(chip - d, 0, chip + 1).start()
            to_twin(chip - d, mine).start()

        @pl.when(chip + d < n_chip)
        def _():
            along(chip + d, 1, chip).wait_recv()
            if onward:
                @pl.when(chip > 0)
                def _():
                    along(chip + d, 1, chip - 1).start()
            to_twin(chip + d, mine).start()

    def both_sides(d, body):
        def side(k):
            s = chip + d * (2 * k - 1)

            @pl.when((s >= 0) & (s < n_chip))
            def _():
                body(s)
        each(0, 2, side)

    def take(s):
        to_twin(s, others).wait_recv()
        prepare_first(s)

    def middle(d):
        receive(d, True)

        def body(s):
            take(s)
            tile(s, row)
        both_sides(d, body)
    each(1, n_chip - 1, middle)

    last = n_chip - 1

    def near(body):
        def check(s):
            @pl.when((s - chip < last) & (chip - s < last))
            def _():
                body(s)
        each(0, n_chip, check)

    def row_step(p):
        for copy in rows_from(p):
            copy.wait_recv()
        peer = flip(row, p, n_row)
        prepare_second(peer)
        near(lambda s: tile(s, peer))
    each(1, n_row, row_step)

    def hand_on(s):
        partial_to_twin(s).wait_recv()

        @pl.when(s != chip)
        def _():
            stage[s] = (part[s, mine] + other[s]).astype(SENT)
            result_to(s).start()

    near(lambda s: partial_to_twin(s).start())
    near(hand_on)

    receive(last, False)

    def far(s):
        take(s)
        each(0, n_row, lambda r: tile(s, r))
        partial_to_twin(s).start()
        hand_on(s)
    both_sides(last, far)

    out[...] = part[chip, mine] + other[chip]

    def add(d):
        s = (chip + d) % n_chip
        result_from(s).wait_recv()
        out[...] += ret[s].astype(jnp.float32)
    each(1, n_chip, add)
    out[...] *= factor

    def sent(s):
        to_twin(s, mine).wait_send()
        partial_to_twin(s).wait_send()

        @pl.when((s <= chip) & (chip + 1 < n_chip))
        def _():
            along(s, 0, chip).wait_send()

        @pl.when((s >= chip) & (chip > 0))
        def _():
            along(s, 1, chip).wait_send()

        @pl.when(s != chip)
        def _():
            result_to(s).wait_send()
    each(0, n_chip, sent)

    def rows_sent(p):
        for copy in rows_to(p):
            copy.wait_send()
    each(1, n_row, rows_sent)


def per_device(fingerprints, probes):
    rows, features = fingerprints.shape
    width = probes.shape[1]
    n_row, n_chip = lax.axis_size("row"), lax.axis_size("col") // 2
    factor = 1.0 / math.sqrt(rows * n_row * n_chip * 2)
    dma = pltpu.SemaphoreType.DMA
    return pl.pallas_call(
        functools.partial(kernel, n_row, n_chip, factor),
        out_shape=jax.ShapeDtypeStruct((rows, width), jnp.float32),
        in_specs=[pl.BlockSpec(memory_space=pltpu.VMEM)] * 2,
        out_specs=pl.BlockSpec(memory_space=pltpu.VMEM),
        scratch_shapes=[
            pltpu.VMEM((n_chip, 2 * rows, features), jnp.bfloat16),
            pltpu.VMEM((n_row, rows, features), jnp.bfloat16),
            pltpu.VMEM((n_row, rows, width), jnp.bfloat16),
            pltpu.VMEM((n_chip, 2 * rows, width), jnp.float32),
            pltpu.VMEM((n_chip, rows, width), jnp.float32),
            pltpu.VMEM((n_chip, rows, width), SENT),
            pltpu.VMEM((n_chip, rows, width), SENT),
            pltpu.VMEM((n_chip, 2 * rows, 128), jnp.float32),
            pltpu.VMEM((n_row, 8, rows), jnp.float32),
            dma((2, n_chip)), dma((n_chip,)),
            dma((n_chip,)), dma((n_chip,)),
            dma((n_row,)), dma((n_row,)),
            dma((n_row,)), dma((n_row,)),
            dma((n_chip,)), dma((n_chip,)),
            dma((n_chip,)), dma((n_chip,)),
        ],
        compiler_params=pltpu.CompilerParams(
            collective_id=0, has_side_effects=True, vmem_limit_bytes=48 * 1024 * 1024
        ),
    )(fingerprints, probes)


def solution(mesh):
    return jax.shard_map(
        per_device,
        mesh=mesh,
        in_specs=(P(("row", "col"), None), P(("row", "col"), None)),
        out_specs=P(("row", "col"), None),
        check_vma=False,
    )
```

```python
import functools
import math

import jax
import jax.numpy as jnp
from jax import lax
from jax.experimental import pallas as pl
from jax.experimental.pallas import tpu as pltpu
from jax.sharding import PartitionSpec as P

MESH = pl.DeviceIdType.MESH
SENT = jnp.bfloat16
CHUNKS = 2


def flip(index, pattern, size):
    result, weight = 0, 1
    while weight < size:
        result = result + weight * ((index // weight + pattern // weight) % 2)
        weight *= 2
    return result


def kernel(n_row, n_chip, factor, fp, pr, out, slab, cols, cpr, part, other, stage, ret, sq_first, sq_second,
           z_send, z_recv, s_send, s_recv, f_send, f_recv, p_send, p_recv, o_send, o_recv, r_send, r_recv, l_sem):
    rows = fp.shape[0]
    row, col = lax.axis_index("row"), lax.axis_index("col")
    chip, core = col // 2, col % 2
    twin = col + 1 - 2 * core
    mine = pl.ds(pl.multiple_of(core * rows, rows), rows)
    piece = rows // CHUNKS
    others = pl.ds(pl.multiple_of((1 - core) * rows, rows), rows)

    def remote(src, dst, send, recv, where):
        return pltpu.make_async_remote_copy(
            src_ref=src, dst_ref=dst, send_sem=send, recv_sem=recv, device_id=where, device_id_type=MESH
        )

    def chunk(of, h):
        return pl.ds(pl.multiple_of(of * rows + h * piece, piece), piece)

    def along(s, way, chip_to, h):
        place = slab.at[s, chunk(core, h)]
        return remote(place, place, z_send.at[way, s, h], z_recv.at[s, h], (row, 2 * chip_to + core))

    def own_along(way, chip_to, h):
        source = fp.at[pl.ds(pl.multiple_of(h * piece, piece), piece)]
        place = slab.at[chip, chunk(core, h)]
        return remote(source, place, z_send.at[way, chip, h], z_recv.at[chip, h], (row, 2 * chip_to + core))

    def to_twin(s, of, h):
        place = slab.at[s, chunk(of, h)]
        return remote(place, place, s_send.at[s, h], s_recv.at[s, h], (row, twin))

    def own_to_twin(h):
        source = fp.at[pl.ds(pl.multiple_of(h * piece, piece), piece)]
        return remote(source, slab.at[chip, chunk(core, h)], s_send.at[chip, h], s_recv.at[chip, h], (row, twin))

    def rows_to(p):
        peer = flip(row, p, n_row)
        return (
            remote(fp, cols.at[row], f_send.at[p], f_recv.at[p], (peer, col)),
            remote(pr, cpr.at[row], p_send.at[p], p_recv.at[p], (peer, col)),
        )

    def rows_from(p):
        peer = flip(row, p, n_row)
        return (
            remote(fp, cols.at[peer], f_send.at[p], f_recv.at[p], (peer, col)),
            remote(pr, cpr.at[peer], p_send.at[p], p_recv.at[p], (peer, col)),
        )

    def partial_to_twin(s):
        return remote(part.at[s, others], other.at[s], o_send.at[s], o_recv.at[s], (row, twin))

    def result_to(s):
        return remote(stage.at[s], ret.at[chip], r_send.at[s], r_recv.at[chip], (row, 2 * s + core))

    def result_from(s):
        return remote(stage.at[s], ret.at[s], r_send.at[s], r_recv.at[s], (row, 2 * s + core))

    def each(low, high, body):
        def step(i, carry):
            body(i)
            return carry
        lax.fori_loop(low, high, step, 0)

    barrier = pltpu.get_barrier_semaphore()

    def greet(where):
        pl.semaphore_signal(barrier, inc=1, device_id=where, device_id_type=MESH)

    each(1, n_row, lambda p: greet((flip(row, p, n_row), col)))
    each(1, n_chip, lambda d: greet((row, 2 * ((chip + d) % n_chip) + core)))
    greet((row, twin))
    local = (
        pltpu.make_async_copy(fp, slab.at[chip, mine], l_sem.at[0]),
        pltpu.make_async_copy(fp, cols.at[row], l_sem.at[1]),
        pltpu.make_async_copy(pr, cpr.at[row], l_sem.at[2]),
    )
    for copy in local:
        copy.start()
    part[...] = jnp.zeros_like(part)
    pl.semaphore_wait(barrier, n_row - 1 + n_chip - 1 + 1)

    def start_own(h):
        @pl.when(chip + 1 < n_chip)
        def _():
            own_along(0, chip + 1, h).start()

        @pl.when(chip > 0)
        def _():
            own_along(1, chip - 1, h).start()
    each(0, CHUNKS, start_own)
    each(0, CHUNKS, lambda h: own_to_twin(h).start())

    def start_rows(p):
        for copy in rows_to(p):
            copy.start()
    each(1, n_row, start_rows)

    def prepare_first(s):
        values = slab[s].astype(jnp.float32)
        sq_first[s] = jnp.broadcast_to(jnp.sum(values * values, axis=1, keepdims=True), sq_first.shape[1:])

    def prepare_second(r):
        values = cols[r].astype(jnp.float32)
        total = jnp.broadcast_to(jnp.sum(values * values, axis=1, keepdims=True), (rows, 128))
        sq_second[r] = total.T[:8]

    def tile(s, r):
        inner = lax.dot_general(slab[s], cols[r], (((1,), (1,)), ((), ())), preferred_element_type=jnp.float32)
        value = inner / (sq_first[s][:, :1] + sq_second[r][:1] - inner)
        part[s] += jnp.dot(value.astype(jnp.bfloat16), cpr[r], preferred_element_type=jnp.float32)

    for copy in local:
        copy.wait()
    prepare_second(row)
    each(0, CHUNKS, lambda h: to_twin(chip, 1 - core, h).wait_recv())
    prepare_first(chip)
    tile(chip, row)

    def receive(d, onward):
        def one(h):
            @pl.when(chip - d >= 0)
            def _():
                along(chip - d, 0, chip, h).wait_recv()
                if onward:
                    @pl.when(chip + 1 < n_chip)
                    def _():
                        along(chip - d, 0, chip + 1, h).start()
                to_twin(chip - d, core, h).start()

            @pl.when(chip + d < n_chip)
            def _():
                along(chip + d, 1, chip, h).wait_recv()
                if onward:
                    @pl.when(chip > 0)
                    def _():
                        along(chip + d, 1, chip - 1, h).start()
                to_twin(chip + d, core, h).start()
        each(0, CHUNKS, one)

    def both_sides(d, body):
        def side(k):
            s = chip + d * (2 * k - 1)

            @pl.when((s >= 0) & (s < n_chip))
            def _():
                body(s)
        each(0, 2, side)

    def take(s):
        each(0, CHUNKS, lambda h: to_twin(s, 1 - core, h).wait_recv())
        prepare_first(s)

    def middle(d):
        receive(d, True)

        def body(s):
            take(s)
            tile(s, row)
        both_sides(d, body)
    each(1, n_chip - 1, middle)

    last = n_chip - 1

    def near(body):
        def check(s):
            @pl.when((s - chip < last) & (chip - s < last))
            def _():
                body(s)
        each(0, n_chip, check)

    def row_step(p):
        for copy in rows_from(p):
            copy.wait_recv()
        peer = flip(row, p, n_row)
        prepare_second(peer)
        near(lambda s: tile(s, peer))
    each(1, n_row, row_step)

    def hand_on(s):
        partial_to_twin(s).wait_recv()

        @pl.when(s != chip)
        def _():
            stage[s] = (part[s, mine] + other[s]).astype(SENT)
            result_to(s).start()

    near(lambda s: partial_to_twin(s).start())
    near(hand_on)

    receive(last, False)

    def far(s):
        take(s)
        each(0, n_row, lambda r: tile(s, r))
        partial_to_twin(s).start()
        hand_on(s)
    both_sides(last, far)

    out[...] = part[chip, mine] + other[chip]

    def add(d):
        s = (chip + d) % n_chip
        result_from(s).wait_recv()
        out[...] += ret[s].astype(jnp.float32)
    each(1, n_chip, add)
    out[...] *= factor

    def sent(s):
        partial_to_twin(s).wait_send()

        def pieces_sent(h):
            to_twin(s, core, h).wait_send()

            @pl.when((s <= chip) & (chip + 1 < n_chip))
            def _():
                along(s, 0, chip, h).wait_send()

            @pl.when((s >= chip) & (chip > 0))
            def _():
                along(s, 1, chip, h).wait_send()
        each(0, CHUNKS, pieces_sent)

        @pl.when(s != chip)
        def _():
            result_to(s).wait_send()
    each(0, n_chip, sent)

    def rows_sent(p):
        for copy in rows_to(p):
            copy.wait_send()
    each(1, n_row, rows_sent)


def per_device(fingerprints, probes):
    rows, features = fingerprints.shape
    width = probes.shape[1]
    n_row, n_chip = lax.axis_size("row"), lax.axis_size("col") // 2
    factor = 1.0 / math.sqrt(rows * n_row * n_chip * 2)
    dma = pltpu.SemaphoreType.DMA
    return pl.pallas_call(
        functools.partial(kernel, n_row, n_chip, factor),
        out_shape=jax.ShapeDtypeStruct((rows, width), jnp.float32),
        in_specs=[pl.BlockSpec(memory_space=pl.ANY)] * 2,
        out_specs=pl.BlockSpec(memory_space=pltpu.VMEM),
        scratch_shapes=[
            pltpu.VMEM((n_chip, 2 * rows, features), jnp.bfloat16),
            pltpu.VMEM((n_row, rows, features), jnp.bfloat16),
            pltpu.VMEM((n_row, rows, width), jnp.bfloat16),
            pltpu.VMEM((n_chip, 2 * rows, width), jnp.float32),
            pltpu.VMEM((n_chip, rows, width), jnp.float32),
            pltpu.VMEM((n_chip, rows, width), SENT),
            pltpu.VMEM((n_chip, rows, width), SENT),
            pltpu.VMEM((n_chip, 2 * rows, 128), jnp.float32),
            pltpu.VMEM((n_row, 8, rows), jnp.float32),
            dma((2, n_chip, CHUNKS)), dma((n_chip, CHUNKS)),
            dma((n_chip, CHUNKS)), dma((n_chip, CHUNKS)),
            dma((n_row,)), dma((n_row,)),
            dma((n_row,)), dma((n_row,)),
            dma((n_chip,)), dma((n_chip,)),
            dma((n_chip,)), dma((n_chip,)),
            dma((3,)),
        ],
        compiler_params=pltpu.CompilerParams(
            collective_id=0, has_side_effects=True, vmem_limit_bytes=62 * 1024 * 1024
        ),
    )(fingerprints, probes)


def solution(mesh):
    return jax.shard_map(
        per_device,
        mesh=mesh,
        in_specs=(P(("row", "col"), None), P(("row", "col"), None)),
        out_specs=P(("row", "col"), None),
        check_vma=False,
    )
```

```python
import functools
import math

import jax
import jax.numpy as jnp
from jax import lax
from jax.experimental import pallas as pl
from jax.experimental.pallas import tpu as pltpu
from jax.sharding import PartitionSpec as P

MESH = pl.DeviceIdType.MESH
SENT = jnp.bfloat16
CHUNKS = 2
ONE_WAY = ((0, 1), (2, 1), (3, 1), (2, 0), (3, 0), (3, 2))
ONE_WAY_CHIPS = 4


def flip(index, pattern, size):
    result, weight = 0, 1
    while weight < size:
        result = result + weight * ((index // weight + pattern // weight) % 2)
        weight *= 2
    return result


def any_of(pairs, s, t):
    found = (s < 0) & (s > 0)
    for a, b in pairs:
        found = found | ((s == a) & (t == b))
    return found


def kernel(n_row, n_chip, factor, fp, pr, out, slab, cols, cpr, spr, part, other, stage, ret, extra, xstage, xin,
           sq_first, sq_second, q_send, q_recv, t_send, t_recv, x_send, x_recv,
           z_send, z_recv, s_send, s_recv, f_send, f_recv, p_send, p_recv, o_send, o_recv, r_send, r_recv, l_sem):
    rows = fp.shape[0]
    row, col = lax.axis_index("row"), lax.axis_index("col")
    chip, core = col // 2, col % 2
    twin = col + 1 - 2 * core
    mine = pl.ds(pl.multiple_of(core * rows, rows), rows)
    piece = rows // CHUNKS
    others = pl.ds(pl.multiple_of((1 - core) * rows, rows), rows)

    one_way = ONE_WAY if n_chip == ONE_WAY_CHIPS else ()
    probed = sorted({a for a, _ in one_way})
    turned = sorted({b for _, b in one_way})

    def goes(s, t):
        return jnp.logical_not(any_of([(b, a) for a, b in one_way], s, t)) & (s != t)

    def have(s):
        return (s == chip) | goes(s, chip)

    def twice(s):
        return any_of(one_way, s, chip)

    def with_probes(s):
        return any_of([(a, 0) for a in probed], s, 0)

    turns = any_of([(b, 0) for b in turned], chip, 0)

    def remote(src, dst, send, recv, where):
        return pltpu.make_async_remote_copy(
            src_ref=src, dst_ref=dst, send_sem=send, recv_sem=recv, device_id=where, device_id_type=MESH
        )

    def chunk(of, h):
        return pl.ds(pl.multiple_of(of * rows + h * piece, piece), piece)

    def along(s, way, chip_to, h):
        place = slab.at[s, chunk(core, h)]
        return remote(place, place, z_send.at[way, s, h], z_recv.at[s, h], (row, 2 * chip_to + core))

    def own_along(way, chip_to, h):
        source = fp.at[pl.ds(pl.multiple_of(h * piece, piece), piece)]
        place = slab.at[chip, chunk(core, h)]
        return remote(source, place, z_send.at[way, chip, h], z_recv.at[chip, h], (row, 2 * chip_to + core))

    def probes_along(s, way, chip_to):
        place = spr.at[s, mine]
        return remote(place, place, q_send.at[way, s], q_recv.at[s], (row, 2 * chip_to + core))

    def own_probes_along(way, chip_to):
        return remote(pr, spr.at[chip, mine], q_send.at[way, chip], q_recv.at[chip], (row, 2 * chip_to + core))

    def probes_to_twin(s, half):
        place = spr.at[s, half]
        return remote(place, place, t_send.at[s], t_recv.at[s], (row, twin))

    def extra_to(p):
        peer = flip(row, p, n_row)
        return remote(xstage.at[peer], xin.at[p], x_send.at[p], x_recv.at[p], (peer, col))

    def to_twin(s, of, h):
        place = slab.at[s, chunk(of, h)]
        return remote(place, place, s_send.at[s, h], s_recv.at[s, h], (row, twin))

    def own_to_twin(h):
        source = fp.at[pl.ds(pl.multiple_of(h * piece, piece), piece)]
        return remote(source, slab.at[chip, chunk(core, h)], s_send.at[chip, h], s_recv.at[chip, h], (row, twin))

    def rows_to(p):
        peer = flip(row, p, n_row)
        return (
            remote(fp, cols.at[row], f_send.at[p], f_recv.at[p], (peer, col)),
            remote(pr, cpr.at[row], p_send.at[p], p_recv.at[p], (peer, col)),
        )

    def rows_from(p):
        peer = flip(row, p, n_row)
        return (
            remote(fp, cols.at[peer], f_send.at[p], f_recv.at[p], (peer, col)),
            remote(pr, cpr.at[peer], p_send.at[p], p_recv.at[p], (peer, col)),
        )

    def partial_to_twin(s):
        return remote(part.at[s, others], other.at[s], o_send.at[s], o_recv.at[s], (row, twin))

    def result_to(s):
        return remote(stage.at[s], ret.at[chip], r_send.at[s], r_recv.at[chip], (row, 2 * s + core))

    def result_from(s):
        return remote(stage.at[s], ret.at[s], r_send.at[s], r_recv.at[s], (row, 2 * s + core))

    def each(low, high, body):
        def step(i, carry):
            body(i)
            return carry
        lax.fori_loop(low, high, step, 0)

    barrier = pltpu.get_barrier_semaphore()

    def greet(where):
        pl.semaphore_signal(barrier, inc=1, device_id=where, device_id_type=MESH)

    each(1, n_row, lambda p: greet((flip(row, p, n_row), col)))
    each(1, n_chip, lambda d: greet((row, 2 * ((chip + d) % n_chip) + core)))
    greet((row, twin))
    local = (
        pltpu.make_async_copy(fp, slab.at[chip, mine], l_sem.at[0]),
        pltpu.make_async_copy(fp, cols.at[row], l_sem.at[1]),
        pltpu.make_async_copy(pr, cpr.at[row], l_sem.at[2]),
    )
    for copy in local:
        copy.start()
    part[...] = jnp.zeros_like(part)
    extra[...] = jnp.zeros_like(extra)
    pl.semaphore_wait(barrier, n_row - 1 + n_chip - 1 + 1)

    def start_own(h):
        @pl.when((chip + 1 < n_chip) & goes(chip, chip + 1))
        def _():
            own_along(0, chip + 1, h).start()

        @pl.when((chip > 0) & goes(chip, chip - 1))
        def _():
            own_along(1, chip - 1, h).start()
    each(0, CHUNKS, start_own)

    if one_way:
        @pl.when((chip + 1 < n_chip) & goes(chip, chip + 1) & with_probes(chip))
        def _():
            own_probes_along(0, chip + 1).start()

        @pl.when((chip > 0) & goes(chip, chip - 1) & with_probes(chip))
        def _():
            own_probes_along(1, chip - 1).start()
    each(0, CHUNKS, lambda h: own_to_twin(h).start())

    def start_rows(p):
        for copy in rows_to(p):
            copy.start()
    each(1, n_row, start_rows)

    def prepare_first(s):
        values = slab[s].astype(jnp.float32)
        sq_first[s] = jnp.broadcast_to(jnp.sum(values * values, axis=1, keepdims=True), sq_first.shape[1:])

    def prepare_second(r):
        values = cols[r].astype(jnp.float32)
        total = jnp.broadcast_to(jnp.sum(values * values, axis=1, keepdims=True), (rows, 128))
        sq_second[r] = total.T[:8]

    def tile(s, r):
        inner = lax.dot_general(slab[s], cols[r], (((1,), (1,)), ((), ())), preferred_element_type=jnp.float32)
        value = inner / (sq_first[s][:, :1] + sq_second[r][:1] - inner)
        value = value.astype(jnp.bfloat16)
        part[s] += jnp.dot(value, cpr[r], preferred_element_type=jnp.float32)
        if one_way:
            @pl.when(twice(s))
            def _():
                extra[r] += lax.dot_general(
                    value, spr[s], (((0,), (0,)), ((), ())), preferred_element_type=jnp.float32
                )

    for copy in local:
        copy.wait()
    prepare_second(row)
    each(0, CHUNKS, lambda h: to_twin(chip, 1 - core, h).wait_recv())
    prepare_first(chip)
    tile(chip, row)

    def receive(d, onward):
        def moved(s, way, there, inside):
            @pl.when((s >= 0) & (s < n_chip) & goes(s, chip))
            def _():
                def one(h):
                    along(s, way, chip, h).wait_recv()
                    if onward:
                        @pl.when(inside & goes(s, there))
                        def _():
                            along(s, way, there, h).start()
                    to_twin(s, core, h).start()
                each(0, CHUNKS, one)
                if one_way:
                    @pl.when(with_probes(s))
                    def _():
                        probes_along(s, way, chip).wait_recv()
                        if onward:
                            @pl.when(inside & goes(s, there))
                            def _():
                                probes_along(s, way, there).start()
                        probes_to_twin(s, mine).start()
        moved(chip - d, 0, chip + 1, chip + 1 < n_chip)
        moved(chip + d, 1, chip - 1, chip > 0)

    def both_sides(d, body):
        def side(k):
            s = chip + d * (2 * k - 1)

            @pl.when((s >= 0) & (s < n_chip) & goes(s, chip))
            def _():
                body(s)
        each(0, 2, side)

    def take(s):
        each(0, CHUNKS, lambda h: to_twin(s, 1 - core, h).wait_recv())
        prepare_first(s)
        if one_way:
            @pl.when(with_probes(s))
            def _():
                probes_to_twin(s, others).wait_recv()

    def middle(d):
        receive(d, True)

        def body(s):
            take(s)
            tile(s, row)
        both_sides(d, body)
    each(1, n_chip - 1, middle)

    last = n_chip - 1

    def near(body):
        def check(s):
            @pl.when((s - chip < last) & (chip - s < last) & have(s))
            def _():
                body(s)
        each(0, n_chip, check)

    def row_step(p):
        for copy in rows_from(p):
            copy.wait_recv()
        peer = flip(row, p, n_row)
        prepare_second(peer)
        near(lambda s: tile(s, peer))
    each(1, n_row, row_step)

    def hand_on(s):
        partial_to_twin(s).wait_recv()

        @pl.when(s != chip)
        def _():
            stage[s] = (part[s, mine] + other[s]).astype(SENT)
            result_to(s).start()

    near(lambda s: partial_to_twin(s).start())
    near(hand_on)

    receive(last, False)

    def far(s):
        take(s)
        each(0, n_row, lambda r: tile(s, r))
        partial_to_twin(s).start()
    both_sides(last, far)

    if one_way:
        def extra_start(p):
            peer = flip(row, p, n_row)
            xstage[peer] = extra[peer].astype(SENT)
            extra_to(p).start()

        @pl.when(turns)
        def _():
            each(1, n_row, extra_start)
    both_sides(last, hand_on)

    out[...] = part[chip, mine] + other[chip]

    if one_way:
        def extra_add(p):
            extra_to(p).wait_recv()
            out[...] += xin[p].astype(jnp.float32)

        @pl.when(turns)
        def _():
            out[...] += extra[row]
            each(1, n_row, extra_add)

    def add(d):
        s = (chip + d) % n_chip

        @pl.when(goes(chip, s))
        def _():
            result_from(s).wait_recv()
            out[...] += ret[s].astype(jnp.float32)
    each(1, n_chip, add)
    out[...] *= factor

    def left(s, way):
        def pieces(h):
            along(s, way, chip, h).wait_send()
        each(0, CHUNKS, pieces)
        if one_way:
            @pl.when(with_probes(s))
            def _():
                probes_along(s, way, chip).wait_send()

    def sent(s):
        @pl.when(have(s))
        def _():
            partial_to_twin(s).wait_send()
            each(0, CHUNKS, lambda h: to_twin(s, core, h).wait_send())
            if one_way:
                @pl.when(with_probes(s) & (s != chip))
                def _():
                    probes_to_twin(s, mine).wait_send()

            @pl.when((s <= chip) & (chip + 1 < n_chip) & goes(s, chip + 1))
            def _():
                left(s, 0)

            @pl.when((s >= chip) & (chip > 0) & goes(s, chip - 1))
            def _():
                left(s, 1)

            @pl.when(s != chip)
            def _():
                result_to(s).wait_send()
    each(0, n_chip, sent)

    if one_way:
        @pl.when(turns)
        def _():
            each(1, n_row, lambda p: extra_to(p).wait_send())

    def rows_sent(p):
        for copy in rows_to(p):
            copy.wait_send()
    each(1, n_row, rows_sent)


def per_device(fingerprints, probes):
    rows, features = fingerprints.shape
    width = probes.shape[1]
    n_row, n_chip = lax.axis_size("row"), lax.axis_size("col") // 2
    factor = 1.0 / math.sqrt(rows * n_row * n_chip * 2)
    dma = pltpu.SemaphoreType.DMA
    return pl.pallas_call(
        functools.partial(kernel, n_row, n_chip, factor),
        out_shape=jax.ShapeDtypeStruct((rows, width), jnp.float32),
        in_specs=[pl.BlockSpec(memory_space=pl.ANY)] * 2,
        out_specs=pl.BlockSpec(memory_space=pltpu.VMEM),
        scratch_shapes=[
            pltpu.VMEM((n_chip, 2 * rows, features), jnp.bfloat16),
            pltpu.VMEM((n_row, rows, features), jnp.bfloat16),
            pltpu.VMEM((n_row, rows, width), jnp.bfloat16),
            pltpu.VMEM((n_chip, 2 * rows, width), jnp.bfloat16),
            pltpu.VMEM((n_chip, 2 * rows, width), jnp.float32),
            pltpu.VMEM((n_chip, rows, width), jnp.float32),
            pltpu.VMEM((n_chip, rows, width), SENT),
            pltpu.VMEM((n_chip, rows, width), SENT),
            pltpu.VMEM((n_row, rows, width), jnp.float32),
            pltpu.VMEM((n_row, rows, width), SENT),
            pltpu.VMEM((n_row, rows, width), SENT),
            pltpu.VMEM((n_chip, 2 * rows, 128), jnp.float32),
            pltpu.VMEM((n_row, 8, rows), jnp.float32),
            dma((2, n_chip)), dma((n_chip,)),
            dma((n_chip,)), dma((n_chip,)),
            dma((n_row,)), dma((n_row,)),
            dma((2, n_chip, CHUNKS)), dma((n_chip, CHUNKS)),
            dma((n_chip, CHUNKS)), dma((n_chip, CHUNKS)),
            dma((n_row,)), dma((n_row,)),
            dma((n_row,)), dma((n_row,)),
            dma((n_chip,)), dma((n_chip,)),
            dma((n_chip,)), dma((n_chip,)),
            dma((3,)),
        ],
        compiler_params=pltpu.CompilerParams(
            collective_id=0, has_side_effects=True, vmem_limit_bytes=62 * 1024 * 1024
        ),
    )(fingerprints, probes)


def solution(mesh):
    return jax.shard_map(
        per_device,
        mesh=mesh,
        in_specs=(P(("row", "col"), None), P(("row", "col"), None)),
        out_specs=P(("row", "col"), None),
        check_vma=False,
    )
```

```python
import functools
import math

import jax
import jax.numpy as jnp
from jax import lax
from jax.experimental import pallas as pl
from jax.experimental.pallas import tpu as pltpu
from jax.sharding import PartitionSpec as P

MESH = pl.DeviceIdType.MESH
SENT = jnp.bfloat16
CHUNKS = 2


def flip(index, pattern, size):
    result, weight = 0, 1
    while weight < size:
        result = result + weight * ((index // weight + pattern // weight) % 2)
        weight *= 2
    return result


def kernel(n_row, n_chip, factor, fp, pr, out, slab, cols, cpr, part, other, stage, ret, sq_first, sq_second,
           z_send, z_recv, s_send, s_recv, f_send, f_recv, p_send, p_recv, o_send, o_recv, r_send, r_recv, l_sem):
    rows = fp.shape[0]
    row, col = lax.axis_index("row"), lax.axis_index("col")
    chip, core = col // 2, col % 2
    twin = col + 1 - 2 * core
    mine = pl.ds(pl.multiple_of(core * rows, rows), rows)
    piece = rows // CHUNKS
    others = pl.ds(pl.multiple_of((1 - core) * rows, rows), rows)

    def remote(src, dst, send, recv, where):
        return pltpu.make_async_remote_copy(
            src_ref=src, dst_ref=dst, send_sem=send, recv_sem=recv, device_id=where, device_id_type=MESH
        )

    def chunk(of, h):
        return pl.ds(pl.multiple_of(of * rows + h * piece, piece), piece)

    def along(s, way, chip_to, h):
        place = slab.at[s, chunk(core, h)]
        return remote(place, place, z_send.at[way, s, h], z_recv.at[s, h], (row, 2 * chip_to + core))

    def own_along(way, chip_to, h):
        source = fp.at[pl.ds(pl.multiple_of(h * piece, piece), piece)]
        place = slab.at[chip, chunk(core, h)]
        return remote(source, place, z_send.at[way, chip, h], z_recv.at[chip, h], (row, 2 * chip_to + core))

    def to_twin(s, of, h):
        place = slab.at[s, chunk(of, h)]
        return remote(place, place, s_send.at[s, h], s_recv.at[s, h], (row, twin))

    def own_to_twin(h):
        source = fp.at[pl.ds(pl.multiple_of(h * piece, piece), piece)]
        return remote(source, slab.at[chip, chunk(core, h)], s_send.at[chip, h], s_recv.at[chip, h], (row, twin))

    def rows_to(p):
        peer = flip(row, p, n_row)
        return (
            remote(fp, cols.at[row], f_send.at[p], f_recv.at[p], (peer, col)),
            remote(pr, cpr.at[row], p_send.at[p], p_recv.at[p], (peer, col)),
        )

    def rows_from(p):
        peer = flip(row, p, n_row)
        return (
            remote(fp, cols.at[peer], f_send.at[p], f_recv.at[p], (peer, col)),
            remote(pr, cpr.at[peer], p_send.at[p], p_recv.at[p], (peer, col)),
        )

    def partial_to_twin(s):
        return remote(part.at[s, others], other.at[s], o_send.at[s], o_recv.at[s], (row, twin))

    def result_to(s):
        return remote(stage.at[s], ret.at[chip], r_send.at[s], r_recv.at[chip], (row, 2 * s + core))

    def result_from(s):
        return remote(stage.at[s], ret.at[s], r_send.at[s], r_recv.at[s], (row, 2 * s + core))

    def each(low, high, body):
        def step(i, carry):
            body(i)
            return carry
        lax.fori_loop(low, high, step, 0)

    barrier = pltpu.get_barrier_semaphore()

    def greet(where):
        pl.semaphore_signal(barrier, inc=1, device_id=where, device_id_type=MESH)

    each(1, n_row, lambda p: greet((flip(row, p, n_row), col)))
    each(1, n_chip, lambda d: greet((row, 2 * ((chip + d) % n_chip) + core)))
    greet((row, twin))
    local = (
        pltpu.make_async_copy(fp, slab.at[chip, mine], l_sem.at[0]),
        pltpu.make_async_copy(fp, cols.at[row], l_sem.at[1]),
        pltpu.make_async_copy(pr, cpr.at[row], l_sem.at[2]),
    )
    for copy in local:
        copy.start()
    part[...] = jnp.zeros_like(part)
    pl.semaphore_wait(barrier, n_row - 1 + n_chip - 1 + 1)

    def start_own(h):
        @pl.when(chip + 1 < n_chip)
        def _():
            own_along(0, chip + 1, h).start()

        @pl.when(chip > 0)
        def _():
            own_along(1, chip - 1, h).start()
    each(0, CHUNKS, start_own)
    each(0, CHUNKS, lambda h: own_to_twin(h).start())

    def start_rows(p):
        for copy in rows_to(p):
            copy.start()
    each(1, n_row, start_rows)

    def prepare_first(s):
        values = slab[s].astype(jnp.float32)
        sq_first[s] = jnp.broadcast_to(jnp.sum(values * values, axis=1, keepdims=True), sq_first.shape[1:])

    def prepare_second(r):
        values = cols[r].astype(jnp.float32)
        total = jnp.broadcast_to(jnp.sum(values * values, axis=1, keepdims=True), (rows, 128))
        sq_second[r] = total.T[:8]

    def tile(s, r):
        inner = lax.dot_general(slab[s], cols[r], (((1,), (1,)), ((), ())), preferred_element_type=jnp.float32)
        value = inner / (sq_first[s][:, :1] + sq_second[r][:1] - inner)
        part[s] += jnp.dot(value.astype(jnp.bfloat16), cpr[r], preferred_element_type=jnp.float32)

    for copy in local:
        copy.wait()
    prepare_second(row)
    each(0, CHUNKS, lambda h: to_twin(chip, 1 - core, h).wait_recv())
    prepare_first(chip)
    tile(chip, row)

    def receive(d, onward):
        def one(h):
            @pl.when(chip - d >= 0)
            def _():
                along(chip - d, 0, chip, h).wait_recv()
                if onward:
                    @pl.when(chip + 1 < n_chip)
                    def _():
                        along(chip - d, 0, chip + 1, h).start()
                to_twin(chip - d, core, h).start()

            @pl.when(chip + d < n_chip)
            def _():
                along(chip + d, 1, chip, h).wait_recv()
                if onward:
                    @pl.when(chip > 0)
                    def _():
                        along(chip + d, 1, chip - 1, h).start()
                to_twin(chip + d, core, h).start()
        each(0, CHUNKS, one)

    def both_sides(d, body):
        def side(k):
            s = chip + d * (2 * k - 1)

            @pl.when((s >= 0) & (s < n_chip))
            def _():
                body(s)
        each(0, 2, side)

    def take(s):
        each(0, CHUNKS, lambda h: to_twin(s, 1 - core, h).wait_recv())
        prepare_first(s)

    def middle(d):
        receive(d, True)

        def body(s):
            take(s)
            tile(s, row)
        both_sides(d, body)
    each(1, n_chip - 1, middle)

    last = n_chip - 1

    def near(body):
        def check(s):
            @pl.when((s - chip < last) & (chip - s < last))
            def _():
                body(s)
        each(0, n_chip, check)

    def row_step(p):
        for copy in rows_from(p):
            copy.wait_recv()
        peer = flip(row, p, n_row)
        prepare_second(peer)

        @pl.when(p < n_row - 1)
        def _():
            near(lambda s: tile(s, peer))

        @pl.when(p == n_row - 1)
        def _():
            def finish(s):
                tile(s, peer)
                partial_to_twin(s).start()
            near(finish)
    each(1, n_row, row_step)

    def hand_on(s):
        partial_to_twin(s).wait_recv()

        @pl.when(s != chip)
        def _():
            stage[s] = (part[s, mine] + other[s]).astype(SENT)
            result_to(s).start()

    near(hand_on)

    receive(last, False)

    def far(s):
        take(s)
        each(0, n_row, lambda r: tile(s, r))
        partial_to_twin(s).start()
        hand_on(s)
    both_sides(last, far)

    out[...] = part[chip, mine] + other[chip]

    def add(d):
        s = (chip + d) % n_chip
        result_from(s).wait_recv()
        out[...] += ret[s].astype(jnp.float32)
    each(1, n_chip, add)
    out[...] *= factor

    def sent(s):
        partial_to_twin(s).wait_send()

        def pieces_sent(h):
            to_twin(s, core, h).wait_send()

            @pl.when((s <= chip) & (chip + 1 < n_chip))
            def _():
                along(s, 0, chip, h).wait_send()

            @pl.when((s >= chip) & (chip > 0))
            def _():
                along(s, 1, chip, h).wait_send()
        each(0, CHUNKS, pieces_sent)

        @pl.when(s != chip)
        def _():
            result_to(s).wait_send()
    each(0, n_chip, sent)

    def rows_sent(p):
        for copy in rows_to(p):
            copy.wait_send()
    each(1, n_row, rows_sent)


def per_device(fingerprints, probes):
    rows, features = fingerprints.shape
    width = probes.shape[1]
    n_row, n_chip = lax.axis_size("row"), lax.axis_size("col") // 2
    factor = 1.0 / math.sqrt(rows * n_row * n_chip * 2)
    dma = pltpu.SemaphoreType.DMA
    return pl.pallas_call(
        functools.partial(kernel, n_row, n_chip, factor),
        out_shape=jax.ShapeDtypeStruct((rows, width), jnp.float32),
        in_specs=[pl.BlockSpec(memory_space=pl.ANY)] * 2,
        out_specs=pl.BlockSpec(memory_space=pltpu.VMEM),
        scratch_shapes=[
            pltpu.VMEM((n_chip, 2 * rows, features), jnp.bfloat16),
            pltpu.VMEM((n_row, rows, features), jnp.bfloat16),
            pltpu.VMEM((n_row, rows, width), jnp.bfloat16),
            pltpu.VMEM((n_chip, 2 * rows, width), jnp.float32),
            pltpu.VMEM((n_chip, rows, width), jnp.float32),
            pltpu.VMEM((n_chip, rows, width), SENT),
            pltpu.VMEM((n_chip, rows, width), SENT),
            pltpu.VMEM((n_chip, 2 * rows, 128), jnp.float32),
            pltpu.VMEM((n_row, 8, rows), jnp.float32),
            dma((2, n_chip, CHUNKS)), dma((n_chip, CHUNKS)),
            dma((n_chip, CHUNKS)), dma((n_chip, CHUNKS)),
            dma((n_row,)), dma((n_row,)),
            dma((n_row,)), dma((n_row,)),
            dma((n_chip,)), dma((n_chip,)),
            dma((n_chip,)), dma((n_chip,)),
            dma((3,)),
        ],
        compiler_params=pltpu.CompilerParams(
            collective_id=0, has_side_effects=True, vmem_limit_bytes=62 * 1024 * 1024
        ),
    )(fingerprints, probes)


def solution(mesh):
    return jax.shard_map(
        per_device,
        mesh=mesh,
        in_specs=(P(("row", "col"), None), P(("row", "col"), None)),
        out_specs=P(("row", "col"), None),
        check_vma=False,
    )
```

```python
import functools
import math

import jax
import jax.numpy as jnp
from jax import lax
from jax.experimental import pallas as pl
from jax.experimental.pallas import tpu as pltpu
from jax.sharding import PartitionSpec as P

MESH = pl.DeviceIdType.MESH
SENT = jnp.bfloat16
CHUNKS = 2


def flip(index, pattern, size):
    result, weight = 0, 1
    while weight < size:
        result = result + weight * ((index // weight + pattern // weight) % 2)
        weight *= 2
    return result


def kernel(n_row, n_chip, factor, fp, pr, out, slab, cols, cpr, part, other, stage, ret, sq_first, sq_second,
           z_send, z_recv, s_send, s_recv, f_send, f_recv, p_send, p_recv, o_send, o_recv, r_send, r_recv, l_sem):
    rows = fp.shape[0]
    row, col = lax.axis_index("row"), lax.axis_index("col")
    chip, core = col // 2, col % 2
    twin = col + 1 - 2 * core
    mine = pl.ds(pl.multiple_of(core * rows, rows), rows)
    piece = rows // CHUNKS
    others = pl.ds(pl.multiple_of((1 - core) * rows, rows), rows)

    def remote(src, dst, send, recv, where):
        return pltpu.make_async_remote_copy(
            src_ref=src, dst_ref=dst, send_sem=send, recv_sem=recv, device_id=where, device_id_type=MESH
        )

    def chunk(of, h):
        return pl.ds(pl.multiple_of(of * rows + h * piece, piece), piece)

    def along(s, way, chip_to, h):
        place = slab.at[s, chunk(core, h)]
        return remote(place, place, z_send.at[way, s, h], z_recv.at[s, h], (row, 2 * chip_to + core))

    def own_along(way, chip_to, h):
        source = fp.at[pl.ds(pl.multiple_of(h * piece, piece), piece)]
        place = slab.at[chip, chunk(core, h)]
        return remote(source, place, z_send.at[way, chip, h], z_recv.at[chip, h], (row, 2 * chip_to + core))

    def to_twin(s, of, h):
        place = slab.at[s, chunk(of, h)]
        return remote(place, place, s_send.at[s, h], s_recv.at[s, h], (row, twin))

    def own_to_twin(h):
        source = fp.at[pl.ds(pl.multiple_of(h * piece, piece), piece)]
        return remote(source, slab.at[chip, chunk(core, h)], s_send.at[chip, h], s_recv.at[chip, h], (row, twin))

    def rows_to(p):
        peer = flip(row, p, n_row)
        return (
            remote(fp, cols.at[row], f_send.at[p], f_recv.at[p], (peer, col)),
            remote(pr, cpr.at[row], p_send.at[p], p_recv.at[p], (peer, col)),
        )

    def rows_from(p):
        peer = flip(row, p, n_row)
        return (
            remote(fp, cols.at[peer], f_send.at[p], f_recv.at[p], (peer, col)),
            remote(pr, cpr.at[peer], p_send.at[p], p_recv.at[p], (peer, col)),
        )

    def partial_to_twin(s):
        return remote(part.at[s, others], other.at[s], o_send.at[s], o_recv.at[s], (row, twin))

    def result_to(s):
        return remote(stage.at[s], ret.at[chip], r_send.at[s], r_recv.at[chip], (row, 2 * s + core))

    def result_from(s):
        return remote(stage.at[s], ret.at[s], r_send.at[s], r_recv.at[s], (row, 2 * s + core))

    def each(low, high, body):
        def step(i, carry):
            body(i)
            return carry
        lax.fori_loop(low, high, step, 0)

    barrier = pltpu.get_barrier_semaphore()

    def greet(where):
        pl.semaphore_signal(barrier, inc=1, device_id=where, device_id_type=MESH)

    each(1, n_row, lambda p: greet((flip(row, p, n_row), col)))
    each(1, n_chip, lambda d: greet((row, 2 * ((chip + d) % n_chip) + core)))
    greet((row, twin))
    local = (
        pltpu.make_async_copy(fp, slab.at[chip, mine], l_sem.at[0]),
        pltpu.make_async_copy(fp, cols.at[row], l_sem.at[1]),
        pltpu.make_async_copy(pr, cpr.at[row], l_sem.at[2]),
    )
    for copy in local:
        copy.start()
    part[...] = jnp.zeros_like(part)
    pl.semaphore_wait(barrier, n_row - 1 + n_chip - 1 + 1)

    def start_own(h):
        @pl.when(chip + 1 < n_chip)
        def _():
            own_along(0, chip + 1, h).start()

        @pl.when(chip > 0)
        def _():
            own_along(1, chip - 1, h).start()
    each(0, CHUNKS, start_own)
    each(0, CHUNKS, lambda h: own_to_twin(h).start())

    def start_rows(p):
        for copy in rows_to(p):
            copy.start()
    each(1, n_row - 1, start_rows)
    if n_chip < 3:
        start_rows(n_row - 1)

    def prepare_first(s):
        values = slab[s].astype(jnp.float32)
        sq_first[s] = jnp.broadcast_to(jnp.sum(values * values, axis=1, keepdims=True), sq_first.shape[1:])

    def prepare_second(r):
        values = cols[r].astype(jnp.float32)
        total = jnp.broadcast_to(jnp.sum(values * values, axis=1, keepdims=True), (rows, 128))
        sq_second[r] = total.T[:8]

    def tile(s, r):
        inner = lax.dot_general(slab[s], cols[r], (((1,), (1,)), ((), ())), preferred_element_type=jnp.float32)
        value = inner / (sq_first[s][:, :1] + sq_second[r][:1] - inner)
        part[s] += jnp.dot(value.astype(jnp.bfloat16), cpr[r], preferred_element_type=jnp.float32)

    for copy in local:
        copy.wait()
    prepare_second(row)
    each(0, CHUNKS, lambda h: to_twin(chip, 1 - core, h).wait_recv())
    prepare_first(chip)
    tile(chip, row)

    def receive(d, onward):
        def one(h):
            @pl.when(chip - d >= 0)
            def _():
                along(chip - d, 0, chip, h).wait_recv()
                if onward:
                    @pl.when(chip + 1 < n_chip)
                    def _():
                        along(chip - d, 0, chip + 1, h).start()
                to_twin(chip - d, core, h).start()

            @pl.when(chip + d < n_chip)
            def _():
                along(chip + d, 1, chip, h).wait_recv()
                if onward:
                    @pl.when(chip > 0)
                    def _():
                        along(chip + d, 1, chip - 1, h).start()
                to_twin(chip + d, core, h).start()
        each(0, CHUNKS, one)

    def both_sides(d, body):
        def side(k):
            s = chip + d * (2 * k - 1)

            @pl.when((s >= 0) & (s < n_chip))
            def _():
                body(s)
        each(0, 2, side)

    def take(s):
        each(0, CHUNKS, lambda h: to_twin(s, 1 - core, h).wait_recv())
        prepare_first(s)

    def middle(d):
        receive(d, True)

        @pl.when(d == 1)
        def _():
            start_rows(n_row - 1)

        def body(s):
            take(s)
            tile(s, row)
        both_sides(d, body)
    each(1, n_chip - 1, middle)

    last = n_chip - 1

    def near(body):
        def check(s):
            @pl.when((s - chip < last) & (chip - s < last))
            def _():
                body(s)
        each(0, n_chip, check)

    def row_step(p):
        for copy in rows_from(p):
            copy.wait_recv()
        peer = flip(row, p, n_row)
        prepare_second(peer)

        @pl.when(p < n_row - 1)
        def _():
            near(lambda s: tile(s, peer))

        @pl.when(p == n_row - 1)
        def _():
            def finish(s):
                tile(s, peer)
                partial_to_twin(s).start()
            near(finish)
    each(1, n_row, row_step)

    def hand_on(s):
        partial_to_twin(s).wait_recv()

        @pl.when(s != chip)
        def _():
            stage[s] = (part[s, mine] + other[s]).astype(SENT)
            result_to(s).start()

    near(hand_on)

    receive(last, False)

    def far(s):
        take(s)
        each(0, n_row, lambda r: tile(s, r))
        partial_to_twin(s).start()
        hand_on(s)
    both_sides(last, far)

    out[...] = part[chip, mine] + other[chip]

    def add(d):
        s = (chip + d) % n_chip
        result_from(s).wait_recv()
        out[...] += ret[s].astype(jnp.float32)
    each(1, n_chip, add)
    out[...] *= factor

    def sent(s):
        partial_to_twin(s).wait_send()

        def pieces_sent(h):
            to_twin(s, core, h).wait_send()

            @pl.when((s <= chip) & (chip + 1 < n_chip))
            def _():
                along(s, 0, chip, h).wait_send()

            @pl.when((s >= chip) & (chip > 0))
            def _():
                along(s, 1, chip, h).wait_send()
        each(0, CHUNKS, pieces_sent)

        @pl.when(s != chip)
        def _():
            result_to(s).wait_send()
    each(0, n_chip, sent)

    def rows_sent(p):
        for copy in rows_to(p):
            copy.wait_send()
    each(1, n_row, rows_sent)


def per_device(fingerprints, probes):
    rows, features = fingerprints.shape
    width = probes.shape[1]
    n_row, n_chip = lax.axis_size("row"), lax.axis_size("col") // 2
    factor = 1.0 / math.sqrt(rows * n_row * n_chip * 2)
    dma = pltpu.SemaphoreType.DMA
    return pl.pallas_call(
        functools.partial(kernel, n_row, n_chip, factor),
        out_shape=jax.ShapeDtypeStruct((rows, width), jnp.float32),
        in_specs=[pl.BlockSpec(memory_space=pl.ANY)] * 2,
        out_specs=pl.BlockSpec(memory_space=pltpu.VMEM),
        scratch_shapes=[
            pltpu.VMEM((n_chip, 2 * rows, features), jnp.bfloat16),
            pltpu.VMEM((n_row, rows, features), jnp.bfloat16),
            pltpu.VMEM((n_row, rows, width), jnp.bfloat16),
            pltpu.VMEM((n_chip, 2 * rows, width), jnp.float32),
            pltpu.VMEM((n_chip, rows, width), jnp.float32),
            pltpu.VMEM((n_chip, rows, width), SENT),
            pltpu.VMEM((n_chip, rows, width), SENT),
            pltpu.VMEM((n_chip, 2 * rows, 128), jnp.float32),
            pltpu.VMEM((n_row, 8, rows), jnp.float32),
            dma((2, n_chip, CHUNKS)), dma((n_chip, CHUNKS)),
            dma((n_chip, CHUNKS)), dma((n_chip, CHUNKS)),
            dma((n_row,)), dma((n_row,)),
            dma((n_row,)), dma((n_row,)),
            dma((n_chip,)), dma((n_chip,)),
            dma((n_chip,)), dma((n_chip,)),
            dma((3,)),
        ],
        compiler_params=pltpu.CompilerParams(
            collective_id=0, has_side_effects=True, vmem_limit_bytes=62 * 1024 * 1024
        ),
    )(fingerprints, probes)


def solution(mesh):
    return jax.shard_map(
        per_device,
        mesh=mesh,
        in_specs=(P(("row", "col"), None), P(("row", "col"), None)),
        out_specs=P(("row", "col"), None),
        check_vma=False,
    )
```
